32 devices in a mesh: dp: 8 (over z, y), mp: 4 (over x, core).
Axes of the slice: x: 2, y: 2, z: 4, core: 2. Of those that a mesh axis runs over, the one named last changes fastest.
Arguments:
- emb_table: bfloat16 [196608, 128], P(('dp', 'mp')), may hold values from -6 to 6
- dense_feats: bfloat16 [4096, 512], P(('dp', 'mp')), may hold values from -6 to 6
- seq_ids: int32 [32, 10240], P(('dp', 'mp')), may hold values from 0 to 196607, as said below
- seq_lengths: int32 [32, 128], P(('dp', 'mp')), may hold values from 1 to 200, 10240 in all within a row
- event_domain: int32 [32, 128], P(('dp', 'mp')), may hold values from 0 to 2
- in_proj: bfloat16 [640, 512], replicated, may hold values from -0.25 to 0.25
- in_bias: float32 [512], replicated, may hold values from -1.75 to 1.75
- norm_gain: float32 [512], replicated, may hold values from 0.5 to 1.5
- norm_shift: float32 [512], replicated, may hold values from -1.75 to 1.75
- expert_first: bfloat16 [16, 512, 1024], P(None, None, 'mp'), may hold values from -0.25 to 0.25
- expert_second: bfloat16 [16, 1024, 512], P(None, 'mp'), may hold values from -0.75 to 0.75
- gate_inner: bfloat16 [3, 512, 8], replicated, may hold values from -0.1875 to 0.1875
- gate_outer: bfloat16 [3, 512, 2], replicated, may hold values from -0.1875 to 0.1875
- tower_first: bfloat16 [3, 512, 256], replicated, may hold values from -0.25 to 0.25
- tower_first_bias: float32 [3, 256], replicated, may hold values from -1.75 to 1.75
- tower_second: bfloat16 [3, 256], replicated, may hold values from -0.375 to 0.375
- tower_second_bias: float32 [3], replicated, may hold values from -3 to 3
- pred_cotangent: float32 [32, 128], P(('dp', 'mp')), may hold values from -6 to 6
Outputs:
- click_prob: float32 [32, 128], P(('dp', 'mp'))
- grad_dense: float32 [4096, 512], P(('dp', 'mp'))
- grad_table: float32 [196608, 128], P(('dp', 'mp'))
- grad_in_proj: float32 [640, 512], replicated
- grad_in_bias: float32 [512], replicated
- grad_norm_gain: float32 [512], replicated
- grad_norm_shift: float32 [512], replicated
- grad_expert_first: float32 [16, 512, 1024], P(None, None, 'mp')
- grad_expert_second: float32 [16, 1024, 512], P(None, 'mp')
- grad_gate_inner: float32 [3, 512, 8], replicated
- grad_gate_outer: float32 [3, 512, 2], replicated
- grad_tower_first: float32 [3, 512, 256], replicated
- grad_tower_first_bias: float32 [3, 256], replicated
- grad_tower_second: float32 [3, 256], replicated
- grad_tower_second_bias: float32 [3], replicated
The draws below stay inside these ranges and needn't reach their ends.
Inputs may be any that keep to these rules, and one draw needn't show every extreme that they name: In each row of seq_ids, at most 640 IDs lie in any one range of table rows [o * 6144, (o + 1) * 6144); in every draw one such range holds exactly 640 IDs of every row.
All inputs are finite; a program needn't handle non-finite values.
Results may differ from the reference program's by a relative error of at most 0.015.
Values may be sent and summed in bfloat16 or wider, within the bound.
A program may use at most 192 MiB of HBM per device.

```python
import math
import jax
import jax.numpy as jnp
import numpy as np
from jax import lax

D = 512
EMB = 128
DENSE = 512
CONCAT = 640
HIDDEN_SIZE = 1024
TOWER = 256
K_SH = 4
K_DOM = 4
DOMAINS = 3
EXPERTS = 16
EV_DEV = 128
MAX_LEN = 200
ROWS_DEV = 6144
OWNERS = 32
IDS_DEV = 10240
CAP = 640
EVENTS = 4096
VOCAB = 196608


def draw_seq_ids(key, part):
    key = jax.random.fold_in(key, 7)
    full_owner = jax.random.randint(jax.random.fold_in(key, 1), (), 0, OWNERS)
    slot_total = OWNERS * CAP

    def one_device(device):
        dev_key = jax.random.fold_in(key, device + 11)
        key_score, key_mix, key_row = jax.random.split(dev_key, 3)
        slot_index = jnp.arange(slot_total, dtype=jnp.int32)
        scores = jax.random.randint(key_score, (slot_total,), 0, 16384) * slot_total + slot_index
        scores = jnp.where(slot_index // CAP == full_owner, slot_index - slot_total, scores)
        chosen = jnp.argsort(scores, stable=True)[:IDS_DEV].astype(jnp.int32)
        shuffled = jax.random.permutation(key_mix, chosen)
        owner_of = shuffled // CAP
        row_pick = jax.random.randint(key_row, (IDS_DEV,), 0, ROWS_DEV)
        return (owner_of * ROWS_DEV + row_pick).astype(jnp.int32)
    return jax.vmap(one_device)(jnp.arange(OWNERS, dtype=jnp.int32))


def with_ends(result, stream_key, smallest, top_value):
    longest = result.shape.index(max(result.shape))
    spots = []
    for shift in (0, 1):
        where = [jax.random.randint(jax.random.fold_in(stream_key, axis), (), 0, length) for axis, length in enumerate(result.shape)]
        where[longest] = (where[longest] + shift) % result.shape[longest]
        spots.append(tuple(where))
    return result.at[spots[0]].set(smallest).at[spots[1]].set(top_value)


def level_of(own_key, extent, shards, low, top_value):
    factor_of, own = 1.0, jax.random.fold_in(own_key, 6)
    for dim, shards_of in shards:
        heights = jnp.exp(jax.random.uniform(jax.random.fold_in(own, dim), (shards_of,), jnp.float32, low / len(shards), top_value / len(shards)))
        factor_of = factor_of * jnp.repeat(heights, extent[dim] // shards_of).reshape([-1 if axis == dim else 1 for axis in range(len(extent))])
    return factor_of


def cumulative_ranks(number_of, skew):
    loads = [(1 << 20) // math.isqrt(standing ** skew) + 1 for standing in range(1, number_of + 1)]
    deviation = 1 + sum(loads) // (1 << 30)
    return np.cumsum(np.array([max(1, weight // deviation) for weight in loads]))


def ranked(own_key, dims, number_of, skew):
    grid = cumulative_ranks(number_of, skew)
    pick = jax.random.randint(jax.random.fold_in(own_key, 1), dims, 0, int(grid[number_of - 1]))
    rank = jnp.searchsorted(jnp.asarray(grid, jnp.int32), pick, side="right")
    return jax.random.permutation(jax.random.fold_in(own_key, 2), number_of)[rank].astype(jnp.int32)


def length_profile(number_of, total, limit, lean):
    weights = [(1 << 20) // math.isqrt(grade ** lean) + 1 for grade in range(2, number_of + 1)]
    spare, given = total - limit - (number_of - 1), [1] * (number_of - 1)
    while spare > 0:
        candidates = [i for i in range(number_of - 1) if given[i] < limit]
        whole, remaining = sum([weights[i] for i in candidates]), spare
        for i in candidates:
            more = min(limit - given[i], max(1, remaining * weights[i] // whole), spare)
            given[i] = given[i] + more
            spare = spare - more
    return np.array([limit] + given)


def uneven(stream_key, amount, total, reach, skew):
    if amount == 2:
        one = jax.random.randint(stream_key, (), max(1, total - reach), min(reach, total - 1) + 1)
        return jnp.stack([one, total - one])
    tallies = jnp.asarray(length_profile(amount, total, reach, skew), jnp.int32)
    pairs = (amount - 1) // 2
    source_of, sink = tallies[1:1 + 2 * pairs:2], tallies[2:2 + 2 * pairs:2]
    slack = jnp.minimum(source_of - 1, reach - sink)
    passed = jax.random.randint(jax.random.fold_in(stream_key, 1), (pairs,), 0, 1 << 20) % (slack + 1)
    tallies = tallies.at[1:1 + 2 * pairs:2].set(source_of - passed).at[2:2 + 2 * pairs:2].set(sink + passed)
    return tallies[jax.random.permutation(jax.random.fold_in(stream_key, 2), amount)]


def noise(key, dims, scale, bound, cuts=(), kind=jnp.bfloat16):
    gain = level_of(key, dims, cuts, -0.22, 0.18) if cuts else 1.0
    values = jax.random.normal(key, dims, jnp.float32) * scale * gain
    return jnp.minimum(jnp.maximum(values, -bound), bound).astype(kind)


def setup_inputs(seed: int = 0) -> dict:
    arg_keys = jax.random.split(jax.random.key(seed), 19)
    emb_table = noise(arg_keys[0], (VOCAB, EMB), 1.0, 6.0, ((0, 32),))
    dense_feats = noise(arg_keys[1], (EVENTS, DENSE), 1.0, 6.0, ((0, 32),))
    seq_ids = draw_seq_ids(jax.random.fold_in(arg_keys[18], 71), 0)
    seq_lengths = jax.vmap(lambda own: uneven(own, EV_DEV, IDS_DEV, MAX_LEN, 2))(jax.random.split(arg_keys[3], OWNERS)).reshape((OWNERS, EV_DEV)).astype(jnp.int32)
    event_domain = with_ends(ranked(arg_keys[4], (OWNERS, EV_DEV), DOMAINS, 2), jax.random.fold_in(arg_keys[4], 3), 0, DOMAINS - 1).astype(jnp.int32)
    in_proj = noise(arg_keys[5], (CONCAT, D), CONCAT ** -0.5, 0.25)
    in_bias = noise(arg_keys[6], (D,), 0.3, 1.75, (), jnp.float32)
    norm_gain = jnp.clip(1.0 + 0.1 * jax.random.normal(arg_keys[7], (D,), jnp.float32), 0.5, 1.5)
    norm_shift = noise(arg_keys[8], (D,), 0.3, 1.75, (), jnp.float32)
    expert_first = noise(arg_keys[9], (EXPERTS, D, HIDDEN_SIZE), D ** -0.5, 0.25, ((2, 4),))
    expert_second = noise(arg_keys[10], (EXPERTS, HIDDEN_SIZE, D), 64 ** -0.5, 0.75, ((1, 4),))
    gate_inner = noise(arg_keys[11], (DOMAINS, D, K_SH + K_DOM), (2 * D) ** -0.5, 0.1875)
    gate_outer = noise(arg_keys[12], (DOMAINS, D, 2), (2 * D) ** -0.5, 0.1875)
    tower_first = noise(arg_keys[13], (DOMAINS, D, TOWER), D ** -0.5, 0.25)
    tower_first_bias = noise(arg_keys[14], (DOMAINS, TOWER), 0.3, 1.75, (), jnp.float32)
    tower_second = noise(arg_keys[15], (DOMAINS, TOWER), TOWER ** -0.5, 0.375)
    tower_second_bias = noise(arg_keys[16], (DOMAINS,), 0.5, 3.0, (), jnp.float32)
    pred_cotangent = noise(arg_keys[17], (OWNERS, EV_DEV), 1.0, 6.0, ((0, 32),), jnp.float32)
    return dict(emb_table=emb_table, dense_feats=dense_feats, seq_ids=seq_ids, seq_lengths=seq_lengths, event_domain=event_domain, in_proj=in_proj, in_bias=in_bias, norm_gain=norm_gain, norm_shift=norm_shift, expert_first=expert_first, expert_second=expert_second, gate_inner=gate_inner, gate_outer=gate_outer, tower_first=tower_first, tower_first_bias=tower_first_bias, tower_second=tower_second, tower_second_bias=tower_second_bias, pred_cotangent=pred_cotangent)


HIGHEST = lax.Precision.HIGHEST
EPSILON = 1e-05

@jax.custom_vjp
def low(v):
    return lax.optimization_barrier(v.astype(jnp.bfloat16)).astype(jnp.float32)

@jax.custom_vjp
def low_back(v):
    return v

def low_keep(v):
    return (low(v), None)

def low_pass(kept, grad):
    return (grad,)

def back_keep(v):
    return (v, None)

def back_low(kept, grad):
    return (low(grad),)
low.defvjp(low_keep, low_pass)
low_back.defvjp(back_keep, back_low)

def gelu_curve(values):
    return jax.nn.gelu(values, approximate=True)

def norm_rows(row_data, gain_vec, shift_vec):
    center = row_data - lax.optimization_barrier(jnp.mean(row_data, axis=-1, keepdims=True))
    spread = lax.optimization_barrier(jnp.mean(center * center, axis=-1, keepdims=True))
    return center * lax.rsqrt(spread + EPSILON) * gain_vec + shift_vec

def gate_mix(hidden_rows, gate_inner, gate_outer, onehot, shared_count):
    inner_logit = jnp.einsum('rd,kde->rke', hidden_rows, gate_inner, precision=HIGHEST)
    outer_logit = jnp.einsum('rd,kde->rke', hidden_rows, gate_outer, precision=HIGHEST)
    inner_logit = lax.optimization_barrier(jnp.sum(onehot[:, :, None] * inner_logit, axis=1))
    outer_logit = lax.optimization_barrier(jnp.sum(onehot[:, :, None] * outer_logit, axis=1))
    shared_prob = jax.nn.softmax(inner_logit[:, :shared_count], axis=-1)
    domain_prob = jax.nn.softmax(inner_logit[:, shared_count:], axis=-1)
    level_prob = jax.nn.softmax(outer_logit, axis=-1)
    domain_part = (level_prob[:, 1:2] * onehot)[:, :, None] * domain_prob[:, None, :]
    return jnp.concatenate([level_prob[:, 0:1] * shared_prob, domain_part.reshape(onehot.shape[0], -1)], axis=1)

def reference(emb_table, dense_feats, seq_ids, seq_lengths, event_domain, in_proj, in_bias, norm_gain, norm_shift, expert_first, expert_second, gate_inner, gate_outer, tower_first, tower_first_bias, tower_second, tower_second_bias, pred_cotangent):

    def forward(table_f, dense_f, in_proj_f, in_bias_f, gain_f, shift_f, first_f, second_f, inner_f, outer_f, tower_one_f, tower_one_bias_f, tower_two_f, tower_two_bias_f):

        def one_block(pieces):
            blk_ids, blk_len, blk_dom, blk_dense = pieces
            seq_ends = jnp.cumsum(blk_len).astype(jnp.int32)
            pos_event = jnp.searchsorted(seq_ends, jnp.arange(IDS_DEV, dtype=jnp.int32), side='right').astype(jnp.int32)
            picked = table_f[blk_ids.astype(jnp.int32)]
            summed = jax.ops.segment_sum(picked, pos_event, num_segments=EV_DEV, indices_are_sorted=True)
            pooled = summed / jnp.sqrt(blk_len.astype(jnp.float32))[:, None]
            joined = jnp.concatenate([low(pooled), blk_dense], axis=1)
            projected = low_back(jnp.dot(joined, in_proj_f, precision=HIGHEST) + in_bias_f)
            hidden_rows = low(norm_rows(projected, gain_f, shift_f))
            onehot = (blk_dom[:, None] == jnp.arange(DOMAINS, dtype=jnp.int32)[None, :]).astype(jnp.float32)
            gate_coeff = low(gate_mix(hidden_rows, inner_f, outer_f, onehot, K_SH))
            pre_act = low_back(jnp.einsum('rd,edh->erh', hidden_rows, first_f, precision=HIGHEST))
            scaled = low(gelu_curve(pre_act) * gate_coeff.T[:, :, None])
            expert_out = low_back(jnp.einsum('erh,ehd->rd', scaled, second_f, precision=HIGHEST))
            merged = projected + expert_out
            tower_all = jnp.einsum('rd,kdh->rkh', low(merged), tower_one_f, precision=HIGHEST) + tower_one_bias_f[None, :, :]
            tower_pre = low_back(lax.optimization_barrier(jnp.sum(onehot[:, :, None] * tower_all, axis=1)))
            head_row = jnp.dot(onehot, tower_two_f, precision=HIGHEST)
            click_logit = lax.optimization_barrier(jnp.sum(gelu_curve(tower_pre) * head_row, axis=1)) + jnp.dot(onehot, tower_two_bias_f, precision=HIGHEST)
            return jax.nn.sigmoid(click_logit)
        blocks = (seq_ids, seq_lengths, event_domain, dense_f.reshape(OWNERS, EV_DEV, DENSE))
        return lax.map(jax.checkpoint(one_block), blocks)
    floats = (emb_table.astype(jnp.float32), dense_feats.astype(jnp.float32), in_proj.astype(jnp.float32), in_bias, norm_gain, norm_shift, expert_first.astype(jnp.float32), expert_second.astype(jnp.float32), gate_inner.astype(jnp.float32), gate_outer.astype(jnp.float32), tower_first.astype(jnp.float32), tower_first_bias, tower_second.astype(jnp.float32), tower_second_bias)
    click_prob, pullback = jax.vjp(forward, *floats)
    grads = pullback(pred_cotangent)
    return (click_prob, grads[1], grads[0], grads[2], grads[3], grads[4], grads[5], grads[6], grads[7], grads[8], grads[9], grads[10], grads[11], grads[12], grads[13])
```

```python
import functools

import jax
import jax.numpy as jnp
from jax import lax
from jax.experimental import pallas as pl
from jax.experimental.pallas import tpu as pltpu
from jax.sharding import PartitionSpec as P

K_SH = 4
LANES = 128
STREAMS = 8
MIB = 1 << 20


HIGHEST = lax.Precision.HIGHEST
EPSILON = 1e-05


MESH = pl.DeviceIdType.MESH


def greet(targets):
    barrier = pltpu.get_barrier_semaphore()
    for target in targets:
        pl.semaphore_signal(barrier, inc=1, device_id=target, device_id_type=MESH)
    pl.semaphore_wait(barrier, len(targets))


def remote(src, dst, send, recv, target):
    return pltpu.make_async_remote_copy(
        src_ref=src, dst_ref=dst, send_sem=send, recv_sem=recv, device_id=target,
        device_id_type=MESH,
    )


def swap_kernel(dp_size, mp_size, lists_ref, got_ref, send, recv):
    dp, mp = lax.axis_index("dp"), lax.axis_index("mp")
    count = dp_size * mp_size
    me = dp * mp_size + mp
    barrier = pltpu.get_barrier_semaphore()

    def to(k):
        target = lax.rem(me + k, count)
        return target, (target // mp_size, lax.rem(target, mp_size))

    def hail(k, carry):
        pl.semaphore_signal(barrier, inc=1, device_id=to(k)[1], device_id_type=MESH)
        return carry

    lax.fori_loop(1, count, hail, 0)
    pl.semaphore_wait(barrier, count - 1)

    def give(k, carry):
        target, place = to(k)
        remote(lists_ref.at[target], got_ref.at[me], send.at[k], recv.at[k], place).start()
        return carry

    lax.fori_loop(1, count, give, 0)
    got_ref[me] = lists_ref[me]

    def take(k, carry):
        target, place = to(k)
        source = lax.rem(me + count - k, count)
        copy = remote(lists_ref.at[target], got_ref.at[source], send.at[k], recv.at[k], place)
        copy.wait_send()
        copy.wait_recv()
        return carry

    lax.fori_loop(1, count, take, 0)


def swap_lists(lists):
    dp_size, mp_size = lax.axis_size("dp"), lax.axis_size("mp")
    count = dp_size * mp_size
    return pl.pallas_call(
        functools.partial(swap_kernel, dp_size, mp_size),
        out_shape=jax.ShapeDtypeStruct(lists.shape, lists.dtype),
        in_specs=[pl.BlockSpec(memory_space=pltpu.VMEM)],
        out_specs=pl.BlockSpec(memory_space=pltpu.VMEM),
        scratch_shapes=[pltpu.SemaphoreType.DMA((count,)), pltpu.SemaphoreType.DMA((count,))],
        compiler_params=pltpu.CompilerParams(collective_id=0, has_side_effects=True),
    )(lists)


def bucket_kernel(domains, starts_ref, domain_ref, keys_ref, out_ref):
    owners, rows = out_ref.shape[0], out_ref.shape[1]
    lane = lax.broadcasted_iota(jnp.int32, (rows, LANES), 1)
    place = lax.broadcasted_iota(jnp.int32, (rows, LANES), 0) * LANES + lane
    cuts = jnp.zeros((rows, LANES), jnp.float32)
    for k in range(1, domains + 1):
        below = jnp.sum(jnp.where(domain_ref[...] < k, 1.0, 0.0), axis=1, keepdims=True)
        cuts = jnp.where(lane == k, below, cuts)
    cuts = cuts.astype(jnp.int32)

    def one(owner, carry):
        first = starts_ref[owner]
        count = starts_ref[owner + 1] - first
        top = first // LANES
        skip = first - top * LANES
        block = keys_ref[pl.ds(top, rows), :]
        turned = pltpu.roll(block, lax.rem(LANES - skip, LANES), 1)
        below = pltpu.roll(turned, rows - 1, 0)
        keys = jnp.where(place < count, jnp.where(lane < LANES - skip, turned, below), -1)
        out_ref[owner] = jnp.where(place < (rows - 1) * LANES, keys, cuts)
        return carry

    lax.fori_loop(0, owners, one, 0)


def bucket(starts, domain, sorted_keys, owners, used, domains):
    rows = -(-(used + 1) // 8) * 8
    pad = jnp.full((rows * LANES,), -1, jnp.int32)
    keys = jnp.concatenate([sorted_keys, pad]).reshape(-1, LANES)
    return pl.pallas_call(
        functools.partial(bucket_kernel, domains),
        out_shape=jax.ShapeDtypeStruct((owners, rows, LANES), jnp.int32),
        in_specs=[
            pl.BlockSpec(memory_space=pltpu.SMEM),
            pl.BlockSpec(memory_space=pltpu.VMEM),
            pl.BlockSpec(memory_space=pltpu.VMEM),
        ],
        out_specs=pl.BlockSpec(memory_space=pltpu.VMEM),
    )(starts, domain, keys)


def event_hot(event_ref, source, events, used):
    parts = []
    for j in range(used):
        row = event_ref[source, j : j + 1, :]
        parts.append(
            (lax.broadcasted_iota(jnp.int32, (events, LANES), 0) == row).astype(jnp.bfloat16)
        )
    return jnp.concatenate(parts, axis=1) if used > 1 else parts[0]


SOURCES = 4


def pool_kernel(used, row_ref, count_ref, event_ref, table_ref, out_ref, wide, *picked):
    step = pl.program_id(0)
    slots = used * LANES
    rows = table_ref.shape[0]

    @pl.when(step == 0)
    def _():
        height = 512

        def widen(i, carry):
            at = pl.multiple_of(i * height, height)
            wide[pl.ds(at, height), :] = table_ref[pl.ds(at, height), :].astype(jnp.float32)
            return carry

        lax.fori_loop(0, rows // height, widen, 0)
        wide[pl.ds(rows, 8), :] = jnp.zeros((8, LANES), jnp.float32)
        for one in picked:
            one[...] = jnp.zeros_like(one)

    batch = 64
    for n in range(SOURCES):
        source = step * SOURCES + n

        def some(i, carry):
            base = pl.multiple_of(i * batch, batch)
            for j in range(batch):
                row = row_ref[source * slots + base + j]
                picked[n][pl.ds(base + j, 1), :] = wide[pl.ds(row, 1), :]
            return carry

        lax.fori_loop(0, (count_ref[source] + batch - 1) // batch, some, 0)
    for n in range(SOURCES):
        hot = event_hot(event_ref, n, out_ref.shape[3], used)
        out_ref[n % 2, n // 2, 0] = jnp.dot(
            hot, picked[n][...].astype(jnp.bfloat16), preferred_element_type=jnp.float32
        ).astype(out_ref.dtype)


def pool(rows, counts, slot_events, table, events, used):
    sources = counts.shape[0]
    return pl.pallas_call(
        functools.partial(pool_kernel, used),
        out_shape=jax.ShapeDtypeStruct((2, 2, sources // 4, events, LANES), jnp.bfloat16),
        grid=(sources // SOURCES,),
        in_specs=[
            pl.BlockSpec(memory_space=pltpu.SMEM),
            pl.BlockSpec(memory_space=pltpu.SMEM),
            pl.BlockSpec((SOURCES,) + slot_events.shape[1:], lambda s: (s, 0, 0)),
            pl.BlockSpec(table.shape, lambda s: (0, 0)),
        ],
        out_specs=pl.BlockSpec((2, 2, 1, events, LANES), lambda s: (0, 0, s, 0, 0)),
        scratch_shapes=[pltpu.VMEM((table.shape[0] + 8, LANES), jnp.float32)]
        + [pltpu.VMEM((used * LANES, LANES), jnp.float32)] * SOURCES,
        compiler_params=pltpu.CompilerParams(vmem_limit_bytes=32 * MIB),
    )(rows, counts, slot_events, table)


def spread_kernel(used, row_ref, count_ref, event_ref, grad_ref, out_ref, *scratch):
    sums, wide = scratch[:STREAMS], scratch[STREAMS:]
    at_step = pl.program_id(0)
    slots = used * LANES
    rows = out_ref.shape[0]
    step = 512

    @pl.when(at_step == 0)
    def _():
        def clear(i, carry):
            at = pl.multiple_of(i * step, step)
            for k in range(STREAMS):
                sums[k][pl.ds(at, step), :] = jnp.zeros((step, LANES), jnp.float32)
            return carry

        lax.fori_loop(0, rows // step, clear, 0)
        for k in range(STREAMS):
            sums[k][pl.ds(rows, 8), :] = jnp.zeros((8, LANES), jnp.float32)

    for n in range(SOURCES):
        hot = event_hot(event_ref, n, grad_ref.shape[3], used)
        wide[n][...] = lax.dot_general(
            hot, grad_ref[0, n % 2, n // 2], (((0,), (0,)), ((), ())),
            preferred_element_type=jnp.float32,
        )
    batch = 32
    for n in range(SOURCES):
        source = at_step * SOURCES + n

        def some(i, carry):
            base = pl.multiple_of(i * batch, batch)
            for j in range(batch):
                row = row_ref[source * slots + base + j]
                sums[j % STREAMS][pl.ds(row, 1), :] += wide[n][pl.ds(base + j, 1), :]
            return carry

        lax.fori_loop(0, (count_ref[source] + batch - 1) // batch, some, 0)

    @pl.when(at_step == pl.num_programs(0) - 1)
    def _():
        def total(i, carry):
            at = pl.multiple_of(i * step, step)
            here = pl.ds(at, step)
            value = sums[0][here, :]
            for k in range(1, STREAMS):
                value = value + sums[k][here, :]
            out_ref[here, :] = value
            return carry

        lax.fori_loop(0, rows // step, total, 0)


def spread(rows, counts, slot_events, grads, table_rows, used):
    sources = counts.shape[0]
    return pl.pallas_call(
        functools.partial(spread_kernel, used),
        out_shape=jax.ShapeDtypeStruct((table_rows, LANES), jnp.float32),
        grid=(sources // SOURCES,),
        in_specs=[
            pl.BlockSpec(memory_space=pltpu.SMEM),
            pl.BlockSpec(memory_space=pltpu.SMEM),
            pl.BlockSpec((SOURCES,) + slot_events.shape[1:], lambda s: (s, 0, 0)),
            pl.BlockSpec((1,) + grads.shape[1:], lambda s: (s, 0, 0, 0, 0)),
        ],
        out_specs=pl.BlockSpec((table_rows, LANES), lambda s: (0, 0)),
        scratch_shapes=[pltpu.VMEM((table_rows + 8, LANES), jnp.float32)] * STREAMS
        + [pltpu.VMEM((used * LANES, LANES), jnp.float32)] * SOURCES,
        compiler_params=pltpu.CompilerParams(vmem_limit_bytes=48 * MIB),
        cost_estimate=pl.CostEstimate(
            flops=100_000_000_000, bytes_accessed=8 * MIB, transcendentals=0
        ),
    )(rows, counts, slot_events, grads)


GELU_A = 0.7978845608028654
GELU_B = 0.044715


def gelu_pair(x):
    square = x * x
    t = jnp.tanh(x * (GELU_A + (GELU_A * GELU_B) * square))
    half = 0.5 + 0.5 * t
    act = x * half
    slope = half + (act * (1.0 - half)) * (2.0 * GELU_A + (6.0 * GELU_A * GELU_B) * square)
    return act, slope


CHUNK = 512
TILE = 16
NT = (((1,), (1,)), ((), ()))


def expert_pair(first_t, second, rows, dout, coeffs):
    pre = lax.dot_general(first_t, rows, NT, preferred_element_type=jnp.float32)
    d_scaled = lax.dot_general(second, dout, NT, preferred_element_type=jnp.float32)
    hidden = pre.shape[0] // len(coeffs)
    scaled, d_pre = [], []
    for j, coeff in enumerate(coeffs):
        mine = slice(j * hidden, (j + 1) * hidden)
        act, slope = gelu_pair(pre[mine])
        scaled.append((act * coeff).astype(jnp.bfloat16))
        d_pre.append((d_scaled[mine] * coeff * slope).astype(jnp.bfloat16))
    return jnp.concatenate(scaled, axis=0), jnp.concatenate(d_pre, axis=0)


def weights_kernel(shared, cut_ref, rows_hbm, dout_hbm, first_ref, second_ref, *rest):
    if shared:
        shared_first_ref, shared_second_ref, tower_in, joint_in, *rest = rest
        d_first_ref, d_second_ref, tower_out, in_proj_out, small_out, *rest = rest
    else:
        d_first_ref, d_second_ref, *rest = rest
    some_rows, some_dout, first_t, sum_first_t, sum_second, rows_ref, dout_ref, load_sems = rest
    group = pl.program_id(0)
    loads = [
        pltpu.make_async_copy(rows_hbm, rows_ref, load_sems.at[0]),
        pltpu.make_async_copy(dout_hbm, dout_ref, load_sems.at[1]),
    ]

    @pl.when(group == 0)
    def _():
        for load in loads:
            load.start()

    @pl.when(group == (1 if shared else 0))
    def _():
        for load in loads:
            load.wait()

    events, width = dout_ref.shape
    count = first_ref.shape[0]
    blocks = cut_ref.shape[0] // 8
    block = events // blocks

    def all_of_them():
        def copy(i, carry):
            here = pl.ds(pl.multiple_of(i * CHUNK, CHUNK), CHUNK)
            some_rows[here, :] = rows_ref[here, :]
            some_dout[here, :] = dout_ref[here, :]
            return carry

        lax.fori_loop(0, events // CHUNK, copy, 0)
        return jnp.int32(events // CHUNK)

    def of_domain():
        def one_block(b, filled):
            low = cut_ref[b * 8 + group - 1]
            high = cut_ref[b * 8 + group]
            start = low // TILE
            stop = jnp.where(high > low, (high + TILE - 1) // TILE, start)

            def one_tile(t, at):
                source = pl.ds(pl.multiple_of(b * block + t * TILE, TILE), TILE)
                target = pl.ds(pl.multiple_of(at * TILE, TILE), TILE)
                some_rows[target, :] = rows_ref[source, :]
                some_dout[target, :] = dout_ref[source, :]
                return at + 1

            return lax.fori_loop(start, stop, one_tile, filled)

        filled = lax.fori_loop(0, blocks, one_block, jnp.int32(0))
        chunks = (filled * TILE + CHUNK - 1) // CHUNK

        def blank(t, carry):
            target = pl.ds(pl.multiple_of(t * TILE, TILE), TILE)
            some_rows[target, :] = jnp.zeros((TILE, some_rows.shape[1]), jnp.bfloat16)
            some_dout[target, :] = jnp.zeros((TILE, width), jnp.bfloat16)
            return carry

        lax.fori_loop(filled, chunks * (CHUNK // TILE), blank, 0)
        return chunks

    def compute(chunks):
        hidden = second_ref.shape[1]
        for j in range(count):
            first_t[j * hidden : (j + 1) * hidden, :] = first_ref[j].T
        sum_first_t[...] = jnp.zeros_like(sum_first_t)
        sum_second[...] = jnp.zeros_like(sum_second)
        shift = lax.rem(LANES - group * count, LANES)

        def part(i, carry):
            here = pl.ds(pl.multiple_of(i * CHUNK, CHUNK), CHUNK)
            rows = some_rows[here, :width]
            dout = some_dout[here, :]
            coeffs = pltpu.roll(some_rows[here, width:].astype(jnp.float32), shift, 1).T
            for b in range(0, count, 2):
                span = slice(b * hidden, (b + 2) * hidden)
                scaled, d_pre = expert_pair(
                    first_t[span, :],
                    second_ref[b : b + 2].reshape(2 * hidden, width),
                    rows,
                    dout,
                    [coeffs[b + j : b + j + 1, :] for j in range(2)],
                )
                sum_second[span, :] += jnp.dot(scaled, dout, preferred_element_type=jnp.float32)
                sum_first_t[span, :] += jnp.dot(d_pre, rows, preferred_element_type=jnp.float32)
            return carry

        lax.fori_loop(0, chunks, part, 0)
        for j in range(count):
            span = slice(j * hidden, (j + 1) * hidden)
            d_first_ref[j] = sum_first_t[span, :].T
            d_second_ref[j] = sum_second[span, :]

    if shared:

        @pl.when(group == 0)
        def _():
            d_first_ref[...] = shared_first_ref[...]
            d_second_ref[...] = shared_second_ref[...]
            dp_size, _, _, tower_rows, _ = tower_in.shape
            joint_rows = joint_in.shape[3]
            half, in_rows = tower_out.shape[0] // 2, in_proj_out.shape[0]
            for d in range(dp_size):
                for q in range(4):
                    lo, hi = q // 2, q % 2
                    at = d * tower_rows
                    n = min(tower_rows, half - at)
                    if n > 0:
                        tower_out[hi * half + at : hi * half + at + n, lo * LANES : (lo + 1) * LANES] = (
                            tower_in[d, lo, hi, :n].astype(jnp.float32)
                        )
                    lanes = slice(q * LANES, (q + 1) * LANES)
                    at = d * joint_rows
                    part = joint_in[d, lo, hi].astype(jnp.float32)
                    n = max(0, min(joint_rows, in_rows - at))
                    if n > 0:
                        in_proj_out[at : at + n, lanes] = part[:n]
                    m = min(joint_rows, in_rows + small_out.shape[0] - at)
                    if m > n:
                        small_out[at + n - in_rows : at + m - in_rows, lanes] = part[n:m]

        @pl.when(group > 0)
        def _():
            compute(of_domain())
    else:
        compute(lax.cond(group == 0, all_of_them, of_domain))


BLOCK_EVENTS = 4096


def expert_weights(rows, dout, cuts, first, second, shared, in_rows):
    events = rows.shape[0]
    total = None
    per = events // cuts.shape[0]
    for at in range(0, events, BLOCK_EVENTS):
        here = slice(at, min(at + BLOCK_EVENTS, events))
        cut = cuts[here.start // per : here.stop // per]
        part = expert_weights_block(rows[here], dout[here], cut, first, second, shared, in_rows)
        total = part if total is None else (total[0] + part[0], total[1] + part[1])
    return total


def expert_weights_block(rows, dout, cuts, first, second, shared, in_rows):
    events, width = dout.shape
    experts, _, hidden = first.shape
    domains = cuts.shape[1] - 1
    count = experts // (domains + 1)
    cuts = jnp.pad(cuts, ((0, 0), (0, 8 - cuts.shape[1]))).reshape(-1)
    origin = lambda ndim, g: (0,) * ndim
    room = events
    extra = ((domains * width, 2 * LANES), (in_rows, width), (48, width)) if shared else ()
    return pl.pallas_call(
        functools.partial(weights_kernel, bool(shared)),
        out_shape=(
            jax.ShapeDtypeStruct((experts, width, hidden), jnp.float32),
            jax.ShapeDtypeStruct((experts, hidden, width), jnp.float32),
        )
        + tuple(jax.ShapeDtypeStruct(a, jnp.float32) for a in extra),
        grid=(domains + 1,),
        in_specs=[
            pl.BlockSpec(memory_space=pltpu.SMEM),
            pl.BlockSpec(memory_space=pl.ANY),
            pl.BlockSpec(memory_space=pl.ANY),
            pl.BlockSpec((count, width, hidden), lambda g: (g, 0, 0)),
            pl.BlockSpec((count, hidden, width), lambda g: (g, 0, 0)),
        ]
        + [
            pl.BlockSpec(a.shape, functools.partial(origin, a.ndim), pipeline_mode=pl.Buffered(1))
            for a in shared
        ],
        out_specs=(
            pl.BlockSpec((count, width, hidden), lambda g: (g, 0, 0)),
            pl.BlockSpec((count, hidden, width), lambda g: (g, 0, 0)),
        )
        + tuple(pl.BlockSpec(a, functools.partial(origin, 2)) for a in extra),
        scratch_shapes=[
            pltpu.VMEM((room, rows.shape[1]), jnp.bfloat16),
            pltpu.VMEM((room, width), jnp.bfloat16),
            pltpu.VMEM((count * hidden, width), jnp.bfloat16),
            pltpu.VMEM((count * hidden, width), jnp.float32),
            pltpu.VMEM((count * hidden, width), jnp.float32),
            pltpu.VMEM(rows.shape, jnp.bfloat16),
            pltpu.VMEM(dout.shape, jnp.bfloat16),
            pltpu.SemaphoreType.DMA((2,)),
        ],
        compiler_params=pltpu.CompilerParams(vmem_limit_bytes=60 * MIB),
        cost_estimate=pl.CostEstimate(
            flops=8 * events * (experts // 2) * width * hidden,
            bytes_accessed=32 * MIB,
            transcendentals=events * (experts // 2) * hidden,
        ),
    )(cuts, rows, dout, first, second, *shared)


def flip(index, bit):
    return index + bit * (1 - 2 * lax.rem(index // bit, 2))


class Place:
    def __init__(self, dp_size):
        self.dp_size = dp_size
        self.dp, mp = lax.axis_index("dp"), lax.axis_index("mp")
        self.hi, self.lo = mp // 2, lax.rem(mp, 2)
        self.mp = mp
        self.core = (self.dp, 2 * self.hi + 1 - self.lo)
        self.side = (self.dp, 2 * (1 - self.hi) + self.lo)

    def peers(self):
        return [(lax.rem(self.dp + k, self.dp_size), self.mp) for k in range(1, self.dp_size)]


class Everywhere:
    def __init__(self, place, group, buf, send, recv):
        self.place, self.group, self.buf, self.send, self.recv = place, group, buf, send, recv
        self.started = []
        self.keep = pltpu.make_async_copy(group, buf.at[place.dp], send.at[3])
        self.step = 0
        self.waited = set()
        self.kept = False
        self.bits = []
        bit = place.dp_size // 2
        while bit:
            self.bits.append(bit)
            bit //= 2

    def copy(self, block, index, target, source=None):
        source = block if source is None else source
        return remote(source, block, self.send.at[index], self.recv.at[index], target)

    def start(self, block, index, target, source=None):
        copy = self.copy(block, index, target, source)
        copy.start()
        self.started.append(copy)

    def give_own(self):
        p = self.place
        own = self.group.at[p.lo, p.hi]
        self.start(own, 0, p.side)
        self.start(own, 1, p.core)

    def take_group(self):
        p = self.place
        far = self.group.at[p.lo, 1 - p.hi]
        self.copy(far, 0, p.side).wait_recv()
        self.start(far, 2, p.core)
        self.copy(self.group.at[1 - p.lo, p.hi], 1, p.core).wait_recv()
        self.copy(self.group.at[1 - p.lo, 1 - p.hi], 2, p.core).wait_recv()
        self.keep.start()

    def held(self, step):
        sets = [()]
        for bit in self.bits[:step]:
            sets += [s + (bit,) for s in sets]
        return sets

    def at(self, turned):
        index = self.place.dp
        for bit in turned:
            index = flip(index, bit)
        return index

    def give(self, step):
        p = self.place
        bit = self.bits[step]
        for turned in self.held(step):
            self.start(
                self.buf.at[self.at(turned), p.lo],
                3 + sum(turned) + bit,
                (flip(p.dp, bit), p.mp),
                None if turned else self.group.at[p.lo],
            )

    def take(self, step):
        p = self.place
        bit = self.bits[step]
        for turned in self.held(step):
            block = self.buf.at[self.at(turned + (bit,)), p.lo]
            index = 3 + sum(turned) + bit
            self.copy(block, index, (flip(p.dp, bit), p.mp)).wait_recv()
            self.start(block, index + p.dp_size, p.core)

    def advance(self):
        if self.step:
            if self.step > len(self.bits):
                return
            self.take(self.step - 1)
        if self.step < len(self.bits):
            self.give(self.step)
        self.step += 1

    def need(self, turned):
        p = self.place
        if not turned:
            if not self.kept:
                self.keep.wait()
                self.kept = True
        elif turned not in self.waited:
            self.waited.add(turned)
            block = self.buf.at[self.at(turned), 1 - p.lo]
            self.copy(block, 3 + sum(turned) + p.dp_size, p.core).wait_recv()

    def finish(self):
        while self.step <= len(self.bits):
            self.advance()
        for turned in self.held(len(self.bits)):
            self.need(turned)
        for copy in self.started:
            copy.wait_send()

    @staticmethod
    def scratch(dp_size, rows, cols):
        return [pltpu.VMEM((2, 2, rows, cols), jnp.bfloat16)] + [pltpu.SemaphoreType.DMA((3 + 2 * dp_size,))] * 2


class GroupSum:
    def __init__(self, place, parts, near, far_out, far_in, send, recv):
        self.place, self.parts, self.near = place, parts, near
        self.far_out, self.far_in = far_out, far_in
        p = place
        self.copies = [
            remote(parts.at[1 - p.lo, 1 - p.hi], near.at[0], send.at[0], recv.at[0], p.core),
            remote(parts.at[1 - p.lo, p.hi], near.at[1], send.at[1], recv.at[1], p.core),
            remote(far_out, far_in, send.at[2], recv.at[2], p.side),
        ]

    def start(self):
        self.copies[0].start()
        self.copies[1].start()

    def middle(self):
        p = self.place
        self.copies[0].wait_recv()
        self.far_out[...] = (
            self.parts[p.lo, 1 - p.hi].astype(jnp.float32) + self.near[0].astype(jnp.float32)
        ).astype(self.far_out.dtype)
        self.copies[2].start()

    def finish(self):
        p = self.place
        self.copies[1].wait_recv()
        total = self.parts[p.lo, p.hi].astype(jnp.float32) + self.near[1].astype(jnp.float32)
        self.copies[2].wait_recv()
        total = total + self.far_in[...].astype(jnp.float32)
        for copy in self.copies:
            copy.wait_send()
        return total

    @staticmethod
    def scratch(rows, cols, near_type, far_type):
        return [
            pltpu.VMEM((2, rows, cols), near_type),
            pltpu.VMEM((rows, cols), far_type),
            pltpu.VMEM((rows, cols), far_type),
            pltpu.SemaphoreType.DMA((3,)),
            pltpu.SemaphoreType.DMA((3,)),
        ]


class EverywhereSum:
    def __init__(self, place, parts, near_buf, far_out, far_in, dp_out, dp_in, send, recv):
        self.place, self.parts, self.near_buf = place, parts, near_buf
        self.far_out, self.far_in, self.dp_out, self.dp_in = far_out, far_in, dp_out, dp_in
        p = place
        half = p.dp_size // 2
        self.halves = [pl.ds(h * half, half) for h in range(2)]
        self.near, self.far = [], []
        for j, hi in enumerate((1 - p.hi, p.hi)):
            for h, at in enumerate(self.halves):
                n = 2 * j + h
                self.near.append(
                    remote(
                        parts.at[1 - p.lo, hi, at], near_buf.at[j, at], send.at[n], recv.at[n], p.core
                    )
                )
        for h, at in enumerate(self.halves):
            self.far.append(
                remote(far_out.at[at], far_in.at[at], send.at[4 + h], recv.at[4 + h], p.side)
            )
        self.last = [
            remote(dp_out.at[peer[0]], dp_in.at[k], send.at[5 + k], recv.at[5 + k], peer)
            for k, peer in enumerate(p.peers(), 1)
        ]

    def start(self):
        for copy in self.near:
            copy.start()

    def middle(self):
        p = self.place
        for h, at in enumerate(self.halves):
            self.near[h].wait_recv()
            self.far_out[at] = (
                self.parts[p.lo, 1 - p.hi, at].astype(jnp.float32)
                + self.near_buf[0, at].astype(jnp.float32)
            ).astype(self.far_out.dtype)
            self.far[h].start()

    def over_dp(self):
        p = self.place
        for h, at in enumerate(self.halves):
            self.near[2 + h].wait_recv()
            self.far[h].wait_recv()
            self.dp_out[at] = (
                self.parts[p.lo, p.hi, at].astype(jnp.float32)
                + self.near_buf[1, at].astype(jnp.float32)
                + self.far_in[at].astype(jnp.float32)
            ).astype(self.dp_out.dtype)
        for copy in self.last:
            copy.start()

    def finish(self):
        total = self.dp_out[self.place.dp].astype(jnp.float32)
        for k, copy in enumerate(self.last, 1):
            copy.wait_recv()
            total = total + self.dp_in[k].astype(jnp.float32)
        for copy in self.near + self.far + self.last:
            copy.wait_send()
        return total


def sum_scratch(dp_size, rows, cols, near_type, wire):
    return [
        pltpu.VMEM((2, dp_size, rows, cols), near_type),
        pltpu.VMEM((dp_size, rows, cols), wire),
        pltpu.VMEM((dp_size, rows, cols), wire),
        pltpu.VMEM((dp_size, rows, cols), wire),
        pltpu.VMEM((dp_size, rows, cols), wire),
        pltpu.SemaphoreType.DMA((5 + dp_size,)),
        pltpu.SemaphoreType.DMA((5 + dp_size,)),
    ]


def split_dot(left, exact, dims, pieces=2):
    total, rest = None, left
    for _ in range(pieces):
        piece = rest.astype(jnp.bfloat16)
        part = lax.dot_general(piece, exact, dims, preferred_element_type=jnp.float32)
        total = part if total is None else total + part
        rest = rest - piece.astype(jnp.float32)
    return total


NN = (((1,), (0,)), ((), ()))


def masked_softmax(values, mask):
    top = jnp.max(jnp.where(mask, values, -jnp.inf), axis=1, keepdims=True)
    powers = jnp.where(mask, jnp.exp(values - top), 0.0)
    return powers / jnp.sum(powers, axis=1, keepdims=True)


def softmax_grad(prob, grad):
    return prob * (grad - jnp.sum(grad * prob, axis=1, keepdims=True))


def layers_kernel(
    sizes,
    tail_bias_ref, parts_ref, length_ref, domain_ref, cot_ref, dense_ref, in_proj_ref, bias_ref, gain_ref, shift_ref,
    gate_ref, first_hbm, second_hbm, tower_ref, tower_bias_ref, tower_head_ref,
    click_ref, grad_dense_ref, every_row, every_dout, every_grad, every_tower, every_joint,
    *rest,
):
    dp_size, experts, domains, inner, outer, shared = sizes
    shared_first_ref, shared_second_ref = rest[:2] if shared else (None, None)
    scratch = rest[2:] if shared else rest
    group_experts = inner // 2
    events, dense_width = dense_ref.shape
    emb = parts_ref.shape[-1]
    width = bias_ref.shape[1]
    hidden = second_hbm.shape[1]
    tower = tower_ref.shape[2]
    take = iter(scratch)
    some = lambda n: [next(take) for _ in range(n)]
    pool_scratch = some(7)
    row_group, *row_sems = some(3)
    dout_group, *dout_sems = some(3)
    grad_group, *grad_sems = some(3)
    tower_group, *tower_sems = some(3)
    tower_scratch = some(7)
    tower_grad, tower_parts = some(2)
    joint_group, *joint_sems = some(3)
    joint_scratch = some(7)
    joint, joint_parts = some(2)
    if shared:
        first_t, third_sum, load_rows, load_dout, fetch_sems = some(5)
    out_scratch, rows_scratch, coeff_scratch = some(5), some(5), some(5)
    pre, partial, d_rows_part, d_coeff_part, first_ref, second_ref, load_sems = some(7)
    loads = [
        pltpu.make_async_copy(first_hbm, first_ref, load_sems.at[0]),
        pltpu.make_async_copy(second_hbm, second_ref, load_sems.at[1]),
    ]
    for load in loads:
        load.start()
    p = Place(dp_size)
    greet([p.core, p.side] + p.peers())

    down = lax.broadcasted_iota(jnp.int32, (events, events), 0)
    across = lax.broadcasted_iota(jnp.int32, (events, events), 1)
    kind = domain_ref[...].astype(jnp.float32)
    kind_down = jnp.sum(jnp.where(down == across, kind, 0.0), axis=1, keepdims=True)
    before = (kind_down < kind) | ((kind_down == kind) & (down < across))
    rank = jnp.sum(jnp.where(before, 1.0, 0.0), axis=0, keepdims=True)
    spot = down == rank.astype(jnp.int32)
    spot_wide = spot.astype(jnp.float32)
    order = spot.astype(jnp.bfloat16)
    back = spot_wide.T.astype(jnp.bfloat16)
    column = lambda row: jnp.sum(jnp.where(spot, row.astype(jnp.float32), 0.0), axis=1, keepdims=True)
    root_len = jnp.sqrt(column(length_ref[...]))
    domain = column(domain_ref[...])
    cot = column(cot_ref[...])
    is_domain = [domain == float(k) for k in range(domains)]

    def choose(options):
        value = options[-1]
        for k in range(domains - 2, -1, -1):
            value = jnp.where(is_domain[k], options[k], value)
        return value

    dense = jnp.dot(order, dense_ref[...], preferred_element_type=jnp.float32).astype(jnp.bfloat16)
    projected = (
        jnp.dot(dense, in_proj_ref[emb:, :], preferred_element_type=jnp.float32) + bias_ref[...]
    )

    pool_sum = EverywhereSum(p, parts_ref, *pool_scratch)
    pool_sum.start()
    pool_sum.middle()
    pool_sum.over_dp()
    pooled = pool_sum.finish()
    pooled = split_dot_left_exact(order, pooled) / root_len
    pooled = pooled.astype(jnp.bfloat16)
    projected = projected + jnp.dot(
        pooled, in_proj_ref[:emb, :], preferred_element_type=jnp.float32
    )
    center = projected - jnp.mean(projected, axis=1, keepdims=True)
    inverse = lax.rsqrt(jnp.mean(center * center, axis=1, keepdims=True) + EPSILON)
    xhat = center * inverse
    gain = gain_ref[...]
    rows_own = (xhat * gain + shift_ref[...]).astype(jnp.bfloat16)

    lane = lax.broadcasted_iota(jnp.int32, (events, LANES), 1)
    turn = lambda value, by: pltpu.roll(value, by % LANES, 1)
    logits = jnp.dot(rows_own, gate_ref[...], preferred_element_type=jnp.float32)
    inner_at = [k * inner for k in range(domains)]
    outer_at = [domains * inner + k * outer for k in range(domains)]
    inner_logit = choose([turn(logits, -a) for a in inner_at])
    outer_logit = choose([turn(logits, -a) for a in outer_at])
    is_shared = lane < group_experts
    is_own = (lane >= group_experts) & (lane < inner)
    is_level = lane < outer
    shared_prob = masked_softmax(inner_logit, is_shared)
    domain_prob = masked_softmax(inner_logit, is_own)
    level_prob = masked_softmax(outer_logit, is_level)
    level = [jnp.sum(jnp.where(lane == j, level_prob, 0.0), axis=1, keepdims=True) for j in range(2)]
    own_at = [k * group_experts for k in range(domains)]
    coeff_own = level[0] * shared_prob + choose([turn(level[1] * domain_prob, a) for a in own_at])
    row_group[p.lo, p.hi, :, :width] = rows_own
    row_group[p.lo, p.hi, :, width:] = coeff_own.astype(jnp.bfloat16)
    row_blocks = Everywhere(p, row_group, every_row, *row_sems)
    row_blocks.give_own()
    row_blocks.take_group()
    row_blocks.advance()

    group_rows = 4 * events
    batch = 4
    for load in loads:
        load.wait()
    partial[...] = jnp.zeros_like(partial)

    def forward(i, carry):
        base = i * batch
        joint = row_group[...].reshape(group_rows, -1)
        rows = joint[:, :width]
        coeffs = pltpu.roll(joint[:, width:].astype(jnp.float32), lax.rem(LANES - base, LANES), 1)
        scaled = []
        for j in range(batch):
            value = jnp.dot(rows, first_ref[base + j], preferred_element_type=jnp.float32)
            pre[2 * i + j // 2, :, (j % 2) * hidden : (j % 2 + 1) * hidden] = value
            act, _ = gelu_pair(value)
            scaled.append((act * coeffs[:, j : j + 1]).astype(jnp.bfloat16))
        out = jnp.dot(
            jnp.concatenate(scaled, axis=1),
            second_ref[pl.ds(base, batch)].reshape(batch * hidden, width),
            preferred_element_type=jnp.float32,
        )
        partial[...] += out.reshape(partial.shape)
        return carry

    lax.fori_loop(0, experts // batch, forward, 0)
    out_sum = GroupSum(p, partial, *out_scratch)
    out_sum.start()
    row_blocks.advance()
    out_sum.middle()
    expert_out = out_sum.finish()

    merged = projected + expert_out
    merged_low = merged.astype(jnp.bfloat16)
    tower_pre = choose(
        [
            jnp.dot(merged_low, tower_ref[k], preferred_element_type=jnp.float32)
            + tower_bias_ref[k : k + 1, :]
            for k in range(domains)
        ]
    )
    tower_act, tower_slope = gelu_pair(tower_pre)
    heads = tower_head_ref[...].astype(jnp.float32)
    head = choose([heads[k : k + 1, :] for k in range(domains)])
    logit = jnp.sum(tower_act * head, axis=1, keepdims=True) + choose(
        [tail_bias_ref[k] for k in range(domains)]
    )
    click = 1.0 / (1.0 + jnp.exp(-logit))
    click_ref[...] = jnp.sum(jnp.where(spot, click, 0.0), axis=0, keepdims=True)
    d_logit = cot * click * (1.0 - click)
    d_tower = (d_logit * head * tower_slope).astype(jnp.bfloat16)
    zero = jnp.zeros_like(d_tower)
    masked = [jnp.where(is_domain[k], d_tower, zero) for k in range(domains)]
    d_merged = sum(
        lax.dot_general(masked[k], tower_ref[k], NT, preferred_element_type=jnp.float32)
        for k in range(domains)
    )
    d_out = d_merged.astype(jnp.bfloat16)
    dout_group[p.lo, p.hi] = d_out
    dout_blocks = Everywhere(p, dout_group, every_dout, *dout_sems)
    dout_blocks.give_own()
    row_blocks.advance()
    merged_t = merged_low.astype(jnp.float32).T.astype(jnp.bfloat16)
    for k in range(domains):
        tower_grad[k * width : (k + 1) * width, :] = jnp.dot(
            merged_t, masked[k], preferred_element_type=jnp.float32
        )
    half_rows = domains * width // 2
    tower_rows = tower_parts.shape[3]
    for lo in range(2):
        for hi in range(2):
            for d in range(dp_size):
                start, stop = min(d * tower_rows, half_rows), min((d + 1) * tower_rows, half_rows)
                if stop > start:
                    tower_parts[lo, hi, d, : stop - start, :] = tower_grad[
                        hi * half_rows + start : hi * half_rows + stop,
                        lo * LANES : (lo + 1) * LANES,
                    ]
                if stop - start < tower_rows:
                    tower_parts[lo, hi, d, stop - start :, :] = jnp.zeros(
                        (tower_rows - stop + start, LANES), jnp.float32
                    )
    tower_sum = EverywhereSum(p, tower_parts, *tower_scratch)
    tower_sum.start()
    d_tower_bias = [jnp.sum(m.astype(jnp.float32), axis=0, keepdims=True) for m in masked]
    weighted = d_logit * tower_act
    d_tower_two = [
        jnp.sum(jnp.where(is_domain[k], weighted, 0.0), axis=0, keepdims=True)
        for k in range(domains)
    ]
    d_tail_bias = [
        jnp.sum(jnp.where(is_domain[k], d_logit, 0.0), axis=0, keepdims=True)
        for k in range(domains)
    ]
    dout_blocks.take_group()
    dout_blocks.advance()

    d_rows_wide = partial
    d_rows_wide[...] = jnp.zeros_like(d_rows_wide)
    d_coeff_part[...] = jnp.zeros_like(d_coeff_part)

    def backward(i, carry):
        base = i * batch
        joint = row_group[:, :, :, width:].reshape(group_rows, LANES)
        coeffs = pltpu.roll(joint.astype(jnp.float32), lax.rem(LANES - base, LANES), 1)
        dout = dout_group[...].reshape(group_rows, width)
        d_scaled = lax.dot_general(
            dout, second_ref[pl.ds(base, batch)].reshape(batch * hidden, width), NT,
            preferred_element_type=jnp.float32,
        )
        wide_lane = lax.broadcasted_iota(jnp.int32, (group_rows, LANES), 1)
        total, d_coeff = None, jnp.zeros((group_rows, LANES), jnp.float32)
        for j in range(batch):
            mine = d_scaled[:, j * hidden : (j + 1) * hidden]
            act, slope = gelu_pair(pre[2 * i + j // 2, :, (j % 2) * hidden : (j % 2 + 1) * hidden])
            d_coeff = d_coeff + jnp.where(
                wide_lane == base + j, jnp.sum(mine * act, axis=1, keepdims=True), 0.0
            )
            d_pre = (mine * coeffs[:, j : j + 1] * slope).astype(jnp.bfloat16)
            part = lax.dot_general(
                d_pre, first_ref[base + j], NT, preferred_element_type=jnp.float32
            )
            total = part if total is None else total + part
        d_rows_wide[...] += total.reshape(d_rows_wide.shape)
        d_coeff_part[...] += d_coeff.reshape(d_coeff_part.shape)
        return carry

    lax.fori_loop(0, experts // batch, backward, 0)
    d_rows_part[...] = d_rows_wide[...].astype(jnp.bfloat16)
    rows_sum = GroupSum(p, d_rows_part, *rows_scratch)
    coeff_sum = GroupSum(p, d_coeff_part, *coeff_scratch)
    rows_sum.start()
    coeff_sum.start()
    dout_blocks.advance()
    rows_sum.middle()
    coeff_sum.middle()
    tower_sum.middle()
    d_coeff = coeff_sum.finish()

    d_own = choose([turn(d_coeff, -a) for a in own_at])
    d_shared_prob = d_coeff * level[0]
    d_domain_prob = d_own * level[1]
    d_level = jnp.where(
        lane == 0,
        jnp.sum(d_coeff * shared_prob, axis=1, keepdims=True),
        jnp.where(lane == 1, jnp.sum(d_own * domain_prob, axis=1, keepdims=True), 0.0),
    )
    d_inner = softmax_grad(shared_prob, d_shared_prob) + softmax_grad(domain_prob, d_domain_prob)
    d_outer = softmax_grad(level_prob, d_level)
    d_logits = choose(
        [turn(d_inner, a) + turn(d_outer, b) for a, b in zip(inner_at, outer_at)]
    )
    d_gate = split_dot(d_logits.T, rows_own, NN)
    d_rows_gate = split_dot(d_logits, gate_ref[...], NT)
    d_hidden = rows_sum.finish() + d_rows_gate

    d_gain = jnp.sum(d_hidden * xhat, axis=0, keepdims=True)
    d_shift = jnp.sum(d_hidden, axis=0, keepdims=True)
    dx = d_hidden * gain
    d_projected = d_merged + inverse * (
        dx
        - jnp.mean(dx, axis=1, keepdims=True)
        - xhat * jnp.mean(dx * xhat, axis=1, keepdims=True)
    )
    d_projected = d_projected.astype(jnp.bfloat16)
    d_emb = lax.dot_general(
        d_projected, in_proj_ref[:emb, :], NT, preferred_element_type=jnp.float32
    )
    grad_group[p.lo, p.hi] = jnp.dot(
        back, (d_emb / root_len).astype(jnp.bfloat16), preferred_element_type=jnp.float32
    ).astype(jnp.bfloat16)
    grad_blocks = Everywhere(p, grad_group, every_grad, *grad_sems)
    grad_blocks.give_own()
    tower_sum.over_dp()
    row_blocks.advance()
    d_dense = lax.dot_general(
        d_projected, in_proj_ref[emb:, :], NT, preferred_element_type=jnp.float32
    )
    grad_dense_ref[...] = split_dot_left_exact(back, d_dense)
    d_bias = jnp.sum(d_projected.astype(jnp.float32), axis=0, keepdims=True)
    joined_t = jnp.concatenate([pooled, dense], axis=1).astype(jnp.float32).T.astype(jnp.bfloat16)
    d_in_proj = jnp.dot(joined_t, d_projected, preferred_element_type=jnp.float32)
    grad_blocks.take_group()
    grad_blocks.advance()
    dout_blocks.advance()

    narrow = lax.broadcasted_iota(jnp.int32, (1, 2 * tower), 1)
    tail = jnp.zeros((1, 2 * tower), jnp.float32)
    for k in range(domains):
        tail = tail + jnp.where(narrow == k, d_tail_bias[k], 0.0)
    vectors = [d_bias, d_gain, d_shift, jnp.zeros((5, width), jnp.float32)]
    tails = [jnp.concatenate([a, b], axis=1) for a, b in zip(d_tower_bias, d_tower_two)]
    fill = jnp.zeros((8 - 1 - domains, 2 * tower), jnp.float32)
    in_rows = emb + dense_width
    joint[:in_rows, :] = d_in_proj
    joint[in_rows:, :] = jnp.concatenate([d_gate[:32]] + vectors + tails + [tail, fill], axis=0)
    joint_rows, total_rows = joint_parts.shape[3], joint.shape[0]
    for lo in range(2):
        for hi in range(2):
            lanes = slice((2 * lo + hi) * LANES, (2 * lo + hi + 1) * LANES)
            for d in range(dp_size):
                start, stop = min(d * joint_rows, total_rows), min((d + 1) * joint_rows, total_rows)
                if stop > start:
                    joint_parts[lo, hi, d, : stop - start, :] = joint[start:stop, lanes]
                if stop - start < joint_rows:
                    joint_parts[lo, hi, d, stop - start :, :] = jnp.zeros(
                        (joint_rows - stop + start, LANES), jnp.float32
                    )
    joint_sum = EverywhereSum(p, joint_parts, *joint_scratch)
    joint_sum.start()
    tower_group[p.lo, p.hi] = tower_sum.finish().astype(tower_group.dtype)
    tower_blocks = Everywhere(p, tower_group, every_tower, *tower_sems)
    joint_blocks = Everywhere(p, joint_group, every_joint, *joint_sems)
    tower_blocks.give_own()
    joint_sum.middle()

    def after_first():
        joint_sum.over_dp()
        grad_blocks.advance()
        tower_blocks.take_group()
        tower_blocks.advance()

    def after_second():
        grad_blocks.advance()
        tower_blocks.advance()
        joint_group[p.lo, p.hi] = joint_sum.finish().astype(joint_group.dtype)
        joint_blocks.give_own()

    def after_third():
        tower_blocks.advance()
        joint_blocks.take_group()
        joint_blocks.advance()

    between = [after_first, after_second, after_third]
    if shared:
        shared_experts(
            row_blocks, dout_blocks, between, first_ref, first_t, second_ref, pre, third_sum, partial,
            load_rows, load_dout, fetch_sems, shared_first_ref, shared_second_ref, group_experts, width,
        )
    for step in between:
        step()
    for _ in grad_blocks.bits:
        grad_blocks.advance()
        tower_blocks.advance()
        joint_blocks.advance()
    grad_blocks.finish()
    tower_blocks.finish()
    joint_blocks.finish()
    row_blocks.finish()
    dout_blocks.finish()


def shared_experts(
    row_blocks, dout_blocks, between, first_ref, first_t, second_ref, pre, third_sum, spare,
    load_rows, load_dout, fetch_sems, out_first, out_second, count, width,
):
    hidden = second_ref.shape[1]
    group_rows = pre.shape[1]
    pairs = count // 2
    sums = [[pre.at[4 * a + b] for b in range(4)] for a in range(2)]
    sums.append([third_sum.at[b] for b in range(4)])
    for j in range(count):
        first_t[j * hidden : (j + 1) * hidden, :] = first_ref[j].T
    far = row_blocks.bits[0]
    order = row_blocks.held(len(row_blocks.bits))
    depth = 0
    for k in range(len(order) // 2):
        turned = order[2 * k]
        last = max(row_blocks.bits.index(bit) for bit in order[2 * k + 1])
        for blocks in (row_blocks, dout_blocks):
            while blocks.step < last + 2:
                blocks.advance()
        for one in (turned, order[2 * k + 1]):
            row_blocks.need(one)
            dout_blocks.need(one)
        near_dp = row_blocks.at(turned)
        far_dp = flip(near_dp, far)

        def fetch(h):
            index = near_dp + h * (far_dp - near_dp)
            return [
                pltpu.make_async_copy(
                    row_blocks.buf.at[index], load_rows.at[h], fetch_sems.at[0, h]
                ),
                pltpu.make_async_copy(
                    dout_blocks.buf.at[index], load_dout.at[h], fetch_sems.at[1, h]
                ),
            ]

        for h in range(2):
            for copy in fetch(h):
                copy.start()
        into = sums[depth]
        depth += 1
        for one in into:
            one[...] = jnp.zeros(one.shape, jnp.float32)

        def one_group(h, carry):
            for copy in fetch(h):
                copy.wait()
            joint = load_rows[h].reshape(group_rows, -1)
            rows = joint[:, :width]
            coeffs = joint[:, width:].astype(jnp.float32).T
            dout = load_dout[h].reshape(group_rows, width)
            for b in range(pairs):
                span = slice(2 * b * hidden, 2 * (b + 1) * hidden)
                scaled, d_pre = expert_pair(
                    first_t[span, :],
                    second_ref[2 * b : 2 * b + 2].reshape(2 * hidden, width),
                    rows,
                    dout,
                    [coeffs[2 * b + j : 2 * b + j + 1, :] for j in range(2)],
                )
                for target, left, right in (
                    (into[b], scaled, dout), (into[2 + b], d_pre, rows)
                ):
                    spare[...] = jnp.dot(
                        left, right, preferred_element_type=jnp.float32
                    ).reshape(spare.shape)
                    target[...] += spare[...].reshape(target.shape)
            return carry

        lax.fori_loop(0, 2, one_group, 0)
        done = k + 1
        while done % 2 == 0:
            for a, b in zip(sums[depth - 2], sums[depth - 1]):
                a[...] += b[...]
            depth -= 1
            done //= 2
        if between:
            between.pop(0)()
    for b in range(pairs):
        for j in range(2):
            mine = slice(j * hidden, (j + 1) * hidden)
            out_second[2 * b + j] = sums[0][b][mine, :]
            out_first[2 * b + j] = sums[0][2 + b][mine, :].T


def split_dot_left_exact(exact, right, pieces=3):
    total, rest = None, right
    for _ in range(pieces):
        piece = rest.astype(jnp.bfloat16)
        part = jnp.dot(exact, piece, preferred_element_type=jnp.float32)
        total = part if total is None else total + part
        rest = rest - piece.astype(jnp.float32)
    return total


def layers(
    tail_bias, parts, lengths, domain, cot, dense, in_proj, bias, gain, shift, gates, first, second, towers,
    tower_bias, tower_head, domains, inner, outer,
):
    _, _, dp_size, events, emb = parts.shape
    experts, width, hidden = first.shape
    shared = dp_size <= 8 and 4 * events == 2 * hidden == width
    count = inner // 2
    joint_total = in_proj.shape[0] + 48
    joint_rows = -(-(-(-joint_total // dp_size)) // 16) * 16
    tower_rows = -(-(-(-domains * width // 2 // dp_size)) // 16) * 16
    every = lambda cols, kind=jnp.bfloat16: jax.ShapeDtypeStruct((dp_size, 2, 2, events, cols), kind)
    vmem = pl.BlockSpec(memory_space=pltpu.VMEM)
    hbm = pl.BlockSpec(memory_space=pl.ANY)
    return pl.pallas_call(
        functools.partial(layers_kernel, (dp_size, experts, domains, inner, outer, shared)),
        out_shape=(
            jax.ShapeDtypeStruct((1, events), jnp.float32),
            jax.ShapeDtypeStruct(dense.shape, jnp.float32),
            every(width + LANES),
            every(width),
            every(emb),
            jax.ShapeDtypeStruct((dp_size, 2, 2, tower_rows, LANES), jnp.bfloat16),
            jax.ShapeDtypeStruct((dp_size, 2, 2, joint_rows, LANES), jnp.bfloat16),
        )
        + (
            jax.ShapeDtypeStruct((count, width, hidden), jnp.float32),
            jax.ShapeDtypeStruct((count, hidden, width), jnp.float32),
        )
        * shared,
        in_specs=[pl.BlockSpec(memory_space=pltpu.SMEM)] + [vmem] * 10 + [hbm] * 2 + [vmem] * 3,
        out_specs=(vmem,) * 2 + (hbm,) * 5 + (vmem,) * (2 * shared),
        scratch_shapes=sum_scratch(dp_size, events, emb, jnp.bfloat16, jnp.bfloat16)
        + Everywhere.scratch(dp_size, events, width + LANES)
        + Everywhere.scratch(dp_size, events, width)
        + Everywhere.scratch(dp_size, events, emb)
        + Everywhere.scratch(dp_size, tower_rows, LANES)
        + sum_scratch(dp_size, tower_rows, LANES, jnp.float32, jnp.bfloat16)
        + [
            pltpu.VMEM((domains * width, towers.shape[2]), jnp.float32),
            pltpu.VMEM((2, 2, dp_size, tower_rows, LANES), jnp.float32),
        ]
        + Everywhere.scratch(dp_size, joint_rows, LANES)
        + sum_scratch(dp_size, joint_rows, LANES, jnp.float32, jnp.bfloat16)
        + [
            pltpu.VMEM((joint_total, width), jnp.float32),
            pltpu.VMEM((2, 2, dp_size, joint_rows, LANES), jnp.float32),
        ]
        + [
            pltpu.VMEM((count * hidden, width), jnp.bfloat16),
            pltpu.VMEM((4, 4 * events, 2 * hidden), jnp.float32),
            pltpu.VMEM((2, 2, 2, events, width + LANES), jnp.bfloat16),
            pltpu.VMEM((2, 2, 2, events, width), jnp.bfloat16),
            pltpu.SemaphoreType.DMA((2, 2)),
        ]
        * shared
        + GroupSum.scratch(events, width, jnp.float32, jnp.bfloat16)
        + GroupSum.scratch(events, width, jnp.bfloat16, jnp.bfloat16)
        + GroupSum.scratch(events, LANES, jnp.float32, jnp.float32)
        + [
            pltpu.VMEM((experts // 2, 4 * events, 2 * hidden), jnp.float32),
            pltpu.VMEM((2, 2, events, width), jnp.float32),
            pltpu.VMEM((2, 2, events, width), jnp.bfloat16),
            pltpu.VMEM((2, 2, events, LANES), jnp.float32),
            pltpu.VMEM(first.shape, jnp.bfloat16),
            pltpu.VMEM(second.shape, jnp.bfloat16),
            pltpu.SemaphoreType.DMA((2,)),
        ],
        compiler_params=pltpu.CompilerParams(
            collective_id=1, has_side_effects=True, vmem_limit_bytes=62 * MIB
        ),
    )(
        tail_bias, parts, lengths, domain, cot, dense, in_proj, bias.reshape(1, -1),
        gain.reshape(1, -1), shift.reshape(1, -1), gates, first, second, towers, tower_bias, tower_head,
    )


def local(
    emb_table,
    dense_feats,
    seq_ids,
    seq_lengths,
    event_domain,
    in_proj,
    in_bias,
    norm_gain,
    norm_shift,
    expert_first,
    expert_second,
    gate_inner,
    gate_outer,
    tower_first,
    tower_first_bias,
    tower_second,
    tower_second_bias,
    pred_cotangent,
):
    owners = lax.axis_size(("dp", "mp"))
    own_index = lax.axis_index(("dp", "mp"))
    id_list = seq_ids[0]
    id_count = id_list.shape[0]
    rows_own = emb_table.shape[0]
    emb_width = emb_table.shape[1]
    slot_count = 2 * id_count // owners
    events = seq_lengths.shape[1]
    domain_count = gate_inner.shape[0]
    used = -(-slot_count // LANES)
    seq_ends = jnp.cumsum(seq_lengths[0])
    pos_event = jnp.sum(
        (seq_ends[:, None] <= jnp.arange(id_count, dtype=jnp.int32)[None, :]).astype(jnp.int32),
        axis=0,
    )
    sorted_keys = lax.sort(id_list * events + pos_event)
    bounds = jnp.arange(owners + 1, dtype=jnp.int32) * rows_own
    starts = jnp.sum((id_list[None, :] < bounds[:, None]).astype(jnp.int32), axis=1)
    send_keys = bucket(starts, event_domain, sorted_keys, owners, used, domain_count)
    got_keys = swap_lists(send_keys)
    slot_keys = got_keys[:, :used, :]
    live_slot = slot_keys >= 0
    slot_event = jnp.where(live_slot, slot_keys % events, events)
    slot_row = jnp.where(live_slot, slot_keys // events - own_index * rows_own, rows_own)
    slot_row = slot_row.reshape(-1)
    live_count = jnp.sum(live_slot.astype(jnp.int32), axis=(1, 2))
    sums_out = pool(slot_row, live_count, slot_event, emb_table, events, used)
    dp_size = owners // 4
    width = in_proj.shape[1]
    inner, outer = gate_inner.shape[2], gate_outer.shape[2]
    gates = jnp.concatenate(
        [
            gate_inner.transpose(1, 0, 2).reshape(width, -1),
            gate_outer.transpose(1, 0, 2).reshape(width, -1),
        ],
        axis=1,
    )
    gates = jnp.pad(gates, ((0, 0), (0, LANES - gates.shape[1])))
    click_prob, grad_dense, every_row, every_dout, every_grad, every_tower, every_joint, *shared = layers(
        tower_second_bias,
        sums_out,
        seq_lengths,
        event_domain,
        pred_cotangent,
        dense_feats,
        in_proj,
        in_bias,
        norm_gain,
        norm_shift,
        gates,
        expert_first,
        expert_second,
        tower_first,
        tower_first_bias,
        tower_second,
        domain_count,
        inner,
        outer,
    )
    grad_table = spread(slot_row, live_count, slot_event, every_grad, rows_own, used)
    block_cuts = got_keys[:, -1, : domain_count + 1].reshape(dp_size, 2, 2, -1)
    expert_sums = expert_weights(
        every_row.reshape(owners * events, -1),
        every_dout.reshape(owners * events, -1),
        block_cuts.transpose(0, 2, 1, 3).reshape(owners, -1),
        expert_first,
        expert_second,
        [*shared, every_tower, every_joint] if shared else [],
        in_proj.shape[0],
    )
    if shared:
        d_tower, d_in_proj, small = expert_sums[2:]
        d_tower = d_tower.reshape(tower_first.shape)
    else:
        d_joint = every_joint.transpose(0, 3, 1, 2, 4).reshape(-1, width).astype(jnp.float32)
        d_in_proj = d_joint[: in_proj.shape[0]]
        small = d_joint[in_proj.shape[0] : in_proj.shape[0] + 48]
        d_tower = every_tower.transpose(2, 0, 3, 1, 4).reshape(2, -1, tower_first.shape[2])
        d_tower = d_tower[:, : domain_count * width // 2].reshape(tower_first.shape)
        d_tower = d_tower.astype(jnp.float32)
    gate_rows = domain_count * inner
    d_inner = small[:gate_rows].reshape(domain_count, inner, width).transpose(0, 2, 1)
    d_outer = small[gate_rows : gate_rows + domain_count * outer]
    d_outer = d_outer.reshape(domain_count, outer, width).transpose(0, 2, 1)
    tower = tower_first.shape[2]
    return (
        click_prob,
        grad_dense,
        grad_table,
        d_in_proj,
        small[32],
        small[33],
        small[34],
        expert_sums[0],
        expert_sums[1],
        d_inner,
        d_outer,
        d_tower,
        small[40 : 40 + domain_count, :tower],
        small[40 : 40 + domain_count, tower:],
        small[40 + domain_count, :domain_count],
    )


def solution(mesh):
    placed = (
        P(("dp", "mp"), None),
        P(("dp", "mp"), None),
        P(("dp", "mp"), None),
        P(("dp", "mp"), None),
        P(("dp", "mp"), None),
        P(),
        P(),
        P(),
        P(),
        P(None, None, "mp"),
        P(None, "mp", None),
        P(),
        P(),
        P(),
        P(),
        P(),
        P(),
        P(("dp", "mp"), None),
    )
    return jax.shard_map(
        local,
        mesh=mesh,
        in_specs=placed,
        out_specs=(
            P(("dp", "mp"), None),
            P(("dp", "mp"), None),
            P(("dp", "mp"), None),
            P(),
            P(),
            P(),
            P(),
            P(None, None, "mp"),
            P(None, "mp", None),
            P(),
            P(),
            P(),
            P(),
            P(),
            P(),
        ),
        check_vma=False,
    )
```
